1024 devices in a mesh: grp: 16 (over y, core), blk: 64 (over x, z).
Axes of the slice: x: 8, y: 8, z: 8, core: 2. Of those that a mesh axis runs over, the one named last changes fastest.
Arguments:
- tile_values: float32 [65536, 32, 128], P(('grp', 'blk')), may hold values from 0.001 to 0.1
- tile_segments: int32 [65536], P(('grp', 'blk')), may hold values from 0 to 1023, as said below
- tile_rows: int32 [65536], P(('grp', 'blk')), may hold values from 0 to 992, as said below
- tile_counts: int32 [1024], P(('grp', 'blk')), may hold values from 32 to 64, as said below
Outputs:
- row_scales: float32 [1048576], P(('grp', 'blk'))
- column_scales: float32 [1024, 128], P(('grp', 'blk'))
The draws below stay inside these ranges and needn't reach their ends.
Inputs may be any that keep to these rules, and one draw needn't show every extreme that they name: `tile_segments`: every segment is named by a live tile of some device; segment s belongs to group s // 64, and the 64 slots of one device name segments of one group at most 4 times. `tile_rows`: multiples of 32; on each device the first 32 slots name every band once. `tile_counts`: some device has 64 live tiles and some only 32.
All inputs are finite; a program needn't handle non-finite values.
Results may differ from the reference program's by a relative error of at most 0.0003.
Values sent between devices are 32-bit elements; how exact they have to be, the bound alone decides.
A program may use at most 32 MiB of HBM per device.

```python
import math
import jax
import jax.numpy as jnp
from jax import lax

TR = 32
BANDS = 32
TILE_DEV = 64
ITERS = 2
TILES = 65536
CAP = 4
N_GRP = 16
N_BLK = 64


def draw_tile_counts(key, part):
    key = jax.random.fold_in(key, 1)
    device_count = N_GRP * N_BLK
    counts = jax.random.randint(key, (device_count,), BANDS, TILE_DEV + 1)
    picked = jax.random.randint(jax.random.fold_in(key, 9), (), 0, device_count)
    other = (picked + device_count // 2) % device_count
    index = jnp.arange(device_count)
    counts = jnp.where(index == picked, TILE_DEV, counts)
    counts = jnp.where(index == other, BANDS, counts)
    return counts.astype(jnp.int32)


def draw_tile_segments(key, part):
    key = jax.random.fold_in(key, 2)
    device_count = N_GRP * N_BLK
    places = N_GRP * CAP
    keys = jax.random.split(key, device_count)
    perms = jax.vmap(lambda single: jax.random.permutation(single, places))(keys).astype(jnp.int32)
    devices = jnp.arange(device_count, dtype=jnp.int32)
    home = (devices // N_BLK + N_GRP // 2) % N_GRP * CAP
    first = jnp.argmax((perms == home[:, None]).astype(jnp.int32), axis=1).astype(jnp.int32)
    slot = jnp.arange(places, dtype=jnp.int32)[None, :]
    front = perms[:, :1]
    swapped = jnp.where(slot == first[:, None], front, perms)
    swapped = jnp.where(slot == 0, home[:, None], swapped)
    groups = swapped[:, :TILE_DEV] // CAP
    blocks = jax.random.randint(jax.random.fold_in(key, 5), (device_count, TILE_DEV), 0, N_BLK).astype(jnp.int32)
    blocks = blocks.at[:, 0].set(devices % N_BLK)
    return (groups * N_BLK + blocks).reshape(-1).astype(jnp.int32)


def draw_tile_rows(key, part):
    key = jax.random.fold_in(key, 3)
    device_count = N_GRP * N_BLK
    keys = jax.random.split(key, device_count)
    ordered = jax.vmap(lambda single: jax.random.permutation(single, BANDS))(keys)
    extra = jax.random.randint(jax.random.fold_in(key, 7), (device_count, TILE_DEV - BANDS), 0, BANDS)
    bands = jnp.concatenate([ordered.astype(jnp.int32), extra.astype(jnp.int32)], axis=1)
    return (bands * TR).reshape(-1).astype(jnp.int32)


def level_of(stream_key, dims, cuts, low, high):
    gain = 1.0
    for axis_at, parts in cuts:
        steps = jax.random.uniform(jax.random.fold_in(jax.random.fold_in(stream_key, 6), axis_at), (parts,), jnp.float32, low / len(cuts), high / len(cuts))
        gain = gain * jnp.repeat(jnp.exp(steps), dims[axis_at] // parts).reshape((-1,) + (1,) * (len(dims) - 1 - axis_at))
    return gain


def setup_inputs(seed: int = 0) -> dict:
    arg_keys = jax.random.split(jax.random.key(seed), 5)
    return {
        "tile_values": jnp.clip(jnp.exp(math.log(0.1) - 4.6051702 * jax.random.uniform(arg_keys[0], (TILES, TR, 128), jnp.float32) ** level_of(arg_keys[0], (TILES, TR, 128), ((0, 1024),), -0.2, 0.2)), 0.001, 0.1),
        "tile_segments": draw_tile_segments(jax.random.fold_in(arg_keys[4], 71), 0),
        "tile_rows": draw_tile_rows(jax.random.fold_in(arg_keys[4], 71), 0),
        "tile_counts": draw_tile_counts(jax.random.fold_in(arg_keys[4], 71), 0),
    }


def reference(tile_values, tile_segments, tile_rows, tile_counts):
    device_count = N_GRP * N_BLK
    segment_total = device_count
    values_all = tile_values.reshape(device_count, TILE_DEV, TR, 128)
    segment_ids = tile_segments.reshape(device_count, TILE_DEV)
    band_ids = (tile_rows // TR).reshape(device_count, TILE_DEV).astype(jnp.int32)
    slot_index = jnp.arange(TILE_DEV, dtype=jnp.int32)
    live_mask = (slot_index[None, :] < tile_counts[:, None]).astype(jnp.float32)
    target = jnp.float32(BANDS * TR * device_count) / jnp.float32(128 * segment_total)
    scales = jnp.ones((segment_total, 128), jnp.float32)
    band_index = jnp.arange(BANDS, dtype=jnp.int32)
    row_result = None
    for sweep in range(ITERS):
        def row_pass(item):
            values, segs, bands, live = item
            chosen = scales[segs]
            partial_rows = jnp.sum(values * chosen[:, None, :], axis=-1) * live[:, None]
            onehot = (bands[:, None] == band_index[None, :]).astype(jnp.float32)
            sums = jnp.dot(onehot.T, partial_rows, precision=lax.Precision.HIGHEST)
            return 1.0 / sums

        row_result = lax.map(row_pass, (values_all, segment_ids, band_ids, live_mask))

        def column_pass(total, item):
            values, segs, bands, live, rscale = item
            weights = rscale[bands]
            column_part = jnp.sum(values * weights[:, :, None], axis=1) * live[:, None]
            return total + jax.ops.segment_sum(column_part, segs, num_segments=segment_total), None

        column_total, unused = lax.scan(column_pass, jnp.zeros((segment_total, 128), jnp.float32), (values_all, segment_ids, band_ids, live_mask, row_result))
        scales = target / column_total
    return row_result.reshape(device_count * BANDS * TR), scales
```

```python
import functools

import jax
import jax.numpy as jnp
from jax import lax
from jax.experimental import pallas as pl
from jax.experimental.pallas import tpu as pltpu
from jax.sharding import PartitionSpec as P

TR = 32
BANDS = 32
CAP = 4
SUB = 8
LANES = 128
CHUNKS = 8
DIRECT = True
MESH = pl.DeviceIdType.MESH
F32 = jnp.float32
BF16 = jnp.bfloat16


def iota(shape, dim):
    return lax.broadcasted_iota(jnp.int32, shape, dim)


def fiota(shape, dim):
    return iota(shape, dim).astype(F32)


def split(x):
    high = x.astype(BF16)
    rest = x - high.astype(F32)
    mid = rest.astype(BF16)
    low = (rest - mid.astype(F32)).astype(BF16)
    return high, mid, low


def pick(onehot, x, dims):
    return sum(
        lax.dot_general(onehot.astype(BF16), part, (dims, ((), ())), preferred_element_type=F32)
        for part in split(x)
    )


def pick_of(x, onehot, dims):
    return sum(
        lax.dot_general(part, onehot.astype(BF16), (dims, ((), ())), preferred_element_type=F32)
        for part in split(x)
    )


def kernel(
    groups, nx, nz, tiles,
    values_hbm, segments_hbm, rows_hbm, counts_hbm,
    rows_out, columns_out,
    values, segments, bands, counts, parts,
    send_a, recv_a, send_x, recv_x, send_z, recv_z, send_own, recv_own, send_all, recv_all, send_b, recv_b, send_c, recv_c,
    load_sem, small_sem, send_sem, recv_sem,
):
    blocks = nx * nz
    me_g = lax.axis_index("grp")
    me_b = lax.axis_index("blk")
    me_x = me_b // nz
    me_z = me_b % nz
    per = tiles // CHUNKS

    def load(q):
        part = pl.ds(q * per, per)
        return pltpu.make_async_copy(values_hbm.at[part], values.at[part], load_sem.at[q])

    smalls = [
        pltpu.make_async_copy(src, dst, small_sem.at[n])
        for n, (src, dst) in enumerate(((segments_hbm, segments), (rows_hbm, bands), (counts_hbm, counts)))
    ]
    for copy in smalls:
        copy.start()
    for q in range(CHUNKS):
        load(q).start()

    barrier = pltpu.get_barrier_semaphore()

    def others(n, me, act):
        def step(k, carry):
            act(lax.rem(me + k, n))
            return carry

        lax.fori_loop(1, n, step, 0)

    others(groups, me_g, lambda o: pl.semaphore_signal(barrier, inc=1, device_id=(o, me_b), device_id_type=MESH))
    if DIRECT:
        others(blocks, me_b, lambda o: pl.semaphore_signal(barrier, inc=1, device_id=(me_g, o), device_id_type=MESH))
        peers = groups + blocks - 2
    else:
        others(nx, me_x, lambda o: pl.semaphore_signal(barrier, inc=1, device_id=(me_g, o * nz + me_z), device_id_type=MESH))
        others(nz, me_z, lambda o: pl.semaphore_signal(barrier, inc=1, device_id=(me_g, me_x * nz + o), device_id_type=MESH))
        peers = groups + nx + nz - 3

    for copy in smalls:
        copy.wait()

    seg_row = segments[...].astype(F32)
    band_row = bands[...].astype(F32) * (1.0 / TR)
    count = counts[...].astype(F32)
    group_row = jnp.floor(seg_row * (1.0 / blocks))
    block_row = seg_row - group_row * blocks
    square = (tiles, tiles)
    down, along = iota(square, 0), iota(square, 1)

    def column(row):
        return jnp.sum(jnp.where(down == along, row, 0.0), axis=1, keepdims=True)

    group_col = column(group_row)
    band_col = column(band_row)
    same_group = group_col == group_row
    rank_row = jnp.sum(jnp.where(same_group & (down < along), 1.0, 0.0), axis=0, keepdims=True)
    place_row = group_row * SUB + rank_row
    slots = groups * SUB
    place = fiota((slots, tiles), 0)
    live_down = fiota(square, 0) < count
    live_along = fiota((slots, tiles), 1) < count
    same_band = jnp.where((band_col == band_row) & live_down, 1.0, 0.0)
    here = place_row == place
    arrange = jnp.where(here & live_along, 1.0, 0.0)
    arrange_all = jnp.where(here, 1.0, 0.0)
    block_ids = jnp.sum(jnp.where(place_row + float(CAP) == place, block_row, 0.0), axis=1, keepdims=True)

    def row_pass(scaled):
        lane = iota((TR, tiles), 1)
        total = jnp.zeros((TR, tiles), F32)
        for q in range(CHUNKS):
            if scaled is None:
                load(q).wait()
            for t in range(q * per, (q + 1) * per):
                tile = values[t]
                if scaled is not None:
                    tile = tile * scaled[t : t + 1, :]
                total = jnp.where(lane == t, jnp.sum(tile, axis=1, keepdims=True), total)
        return total

    def column_pass(weights):
        for t in range(tiles):
            parts[t : t + 1, :] = jnp.sum(values[t] * weights[:, t : t + 1], axis=0, keepdims=True)
        return pick(arrange, parts[...], ((1,), (0,)))

    def stage(n, me, stage_id, source, target, device, size):
        def act(o):
            pltpu.make_async_remote_copy(
                src_ref=source(o), dst_ref=target(me), send_sem=send_sem.at[stage_id], recv_sem=recv_sem.at[stage_id],
                device_id=device(o), device_id_type=MESH,
            ).start()

        others(n, me, act)

    def finish(n, stage_id, ref, sem):
        whole = ref.at[pl.ds(0, n - 1)]
        pltpu.make_async_copy(whole, whole, sem.at[stage_id]).wait()

    sent = []

    def exchange(n, me, stage_id, source_ref, target_ref, device, split_source=True):
        stage(
            n, me, stage_id,
            (lambda o: source_ref.at[o]) if split_source else (lambda o: source_ref),
            lambda o: target_ref.at[o], device, None,
        )
        finish(n, stage_id, target_ref, recv_sem)
        sent.append((n, stage_id, target_ref))

    in_group = lambda o: (o, me_b)
    in_block = lambda o: (me_g, o)
    in_x = lambda o: (me_g, o * nz + me_z)
    in_z = lambda o: (me_g, me_x * nz + o)

    def reduce_blocks(stage_id, dense):
        if DIRECT:
            send_x[stage_id] = dense.reshape(blocks, 1, LANES)
            recv_x[stage_id, me_b] = send_x[stage_id, me_b]
            exchange(blocks, me_b, stage_id, send_x.at[stage_id], recv_x.at[stage_id], in_block)
            return jnp.sum(recv_x[stage_id], axis=0)
        send_x[stage_id] = dense.reshape(nx, nz, LANES)
        recv_x[stage_id, me_x] = send_x[stage_id, me_x]
        exchange(nx, me_x, stage_id, send_x.at[stage_id], recv_x.at[stage_id], in_x)
        mine = jnp.sum(recv_x[stage_id], axis=0)
        send_z[stage_id] = mine.reshape(nz, 1, LANES)
        recv_z[stage_id, me_z] = send_z[stage_id, me_z]
        exchange(nz, me_z, stage_id + 2, send_z.at[stage_id], recv_z.at[stage_id], in_z)
        return jnp.sum(recv_z[stage_id], axis=0)

    def gather_blocks(own):
        send_own[...] = own
        if DIRECT:
            recv_own[me_b] = own
            exchange(blocks, me_b, 4, send_own, recv_own, in_block, False)
            return recv_own[...].reshape(blocks, LANES)
        recv_own[me_z] = own
        exchange(nz, me_z, 4, send_own, recv_own, in_z, False)
        line = recv_own[...].reshape(nz, LANES)
        send_all[...] = line
        recv_all[me_x] = line
        exchange(nx, me_x, 5, send_all, recv_all, in_x, False)
        return recv_all[...].reshape(blocks, LANES)

    target = float(BANDS * TR) / LANES

    sums = row_pass(None)
    weights = 1.0 / pick_of(sums, same_band, ((1,), (0,)))
    arranged = column_pass(weights) + block_ids * jnp.where(iota((slots, 1), 0) % SUB >= CAP, 1.0, 0.0)
    send_a[...] = arranged.reshape(groups, SUB, LANES)
    recv_a[me_g] = send_a[me_g]
    pl.semaphore_wait(barrier, peers)
    exchange(groups, me_g, 6, send_a, recv_a, in_group)

    got = recv_a[...].reshape(slots, LANES)
    ids = pltpu.roll(got, slots - CAP, 0)
    named = jnp.where((ids == fiota((slots, LANES), 1)) & (iota((slots, LANES), 0) % SUB < CAP), 1.0, 0.0)
    dense = pick(named, got, ((0,), (0,)))[:blocks]
    scale = target / reduce_blocks(0, dense)
    scales = gather_blocks(scale)
    reply = pick(named[:, :blocks], scales, ((1,), (0,)))
    send_b[...] = reply.reshape(groups, SUB, LANES)
    recv_b[me_g] = send_b[me_g]
    exchange(groups, me_g, 7, send_b, recv_b, in_group)
    chosen = pick(arrange_all, recv_b[...].reshape(slots, LANES), ((0,), (0,)))

    sums = row_pass(chosen)
    weights = 1.0 / pick_of(sums, same_band, ((1,), (0,)))
    send_c[...] = column_pass(weights).reshape(groups, SUB, LANES)
    recv_c[me_g] = send_c[me_g]
    exchange(groups, me_g, 8, send_c, recv_c, in_group)
    dense = pick(named, recv_c[...].reshape(slots, LANES), ((0,), (0,)))[:blocks]
    columns_out[...] = target / reduce_blocks(1, dense)

    fold = LANES // TR
    lines = BANDS // fold
    wide = jnp.concatenate([sums] * fold, axis=0)
    lane_part = iota((lines, LANES), 1) // TR
    band_sums = jnp.zeros((lines, LANES), F32)
    for m in range(fold):
        members = jnp.where(
            (band_row == fiota((lines, tiles), 0) * fold + m) & (fiota((lines, tiles), 1) < count), 1.0, 0.0
        )
        band_sums = jnp.where(lane_part == m, pick(members, wide, ((1,), (1,))), band_sums)
    rows_out[...] = 1.0 / band_sums

    for n, stage_id, ref in sent:
        finish(n, stage_id, ref, send_sem)


def per_device(nx, nz, tile_values, tile_segments, tile_rows, tile_counts):
    groups = lax.axis_size("grp")
    blocks = lax.axis_size("blk")
    tiles = tile_values.shape[0]
    slots = groups * SUB
    anywhere = pl.BlockSpec(memory_space=pl.ANY)
    if DIRECT:
        x_buf = [pltpu.VMEM((2, blocks, 1, LANES), F32)] * 2
        z_buf = [pltpu.VMEM((2, nz, 1, LANES), F32)] * 2
        own_buf = [pltpu.VMEM((1, LANES), F32), pltpu.VMEM((blocks, 1, LANES), F32)]
    else:
        x_buf = [pltpu.VMEM((2, nx, nz, LANES), F32)] * 2
        z_buf = [pltpu.VMEM((2, nz, 1, LANES), F32)] * 2
        own_buf = [pltpu.VMEM((1, LANES), F32), pltpu.VMEM((nz, 1, LANES), F32)]
    all_buf = [pltpu.VMEM((nz, LANES), F32), pltpu.VMEM((nx, nz, LANES), F32)]
    group_buf = pltpu.VMEM((groups, SUB, LANES), F32)
    rows, columns = pl.pallas_call(
        functools.partial(kernel, groups, nx, nz, tiles),
        out_shape=(
            jax.ShapeDtypeStruct((BANDS * TR // LANES, LANES), F32),
            jax.ShapeDtypeStruct((1, LANES), F32),
        ),
        in_specs=[anywhere] * 4,
        out_specs=(pl.BlockSpec(memory_space=pltpu.VMEM),) * 2,
        scratch_shapes=[
            pltpu.VMEM((tiles, TR, LANES), F32),
            pltpu.VMEM((1, tiles), jnp.int32),
            pltpu.VMEM((1, tiles), jnp.int32),
            pltpu.VMEM((1, 1), jnp.int32),
            pltpu.VMEM((tiles, LANES), F32),
            group_buf, group_buf,
            *x_buf, *z_buf, *own_buf, *all_buf,
            group_buf, group_buf, group_buf, group_buf,
            pltpu.SemaphoreType.DMA((CHUNKS,)),
            pltpu.SemaphoreType.DMA((3,)),
            pltpu.SemaphoreType.DMA((9,)),
            pltpu.SemaphoreType.DMA((9,)),
        ],
        compiler_params=pltpu.CompilerParams(collective_id=0, has_side_effects=True, vmem_limit_bytes=32 * 1024 * 1024),
    )(
        tile_values,
        tile_segments.reshape(1, tiles),
        tile_rows.reshape(1, tiles),
        tile_counts.reshape(1, 1),
    )
    return rows.reshape(BANDS * TR), columns


def solution(mesh):
    blocks = mesh.shape["blk"]
    nz = 8
    nx = blocks // nz
    placed = (
        P(("grp", "blk"), None, None),
        P(("grp", "blk")),
        P(("grp", "blk")),
        P(("grp", "blk")),
    )
    return jax.shard_map(
        functools.partial(per_device, nx, nz),
        mesh=mesh,
        in_specs=placed,
        out_specs=(P(("grp", "blk")), P(("grp", "blk"), None)),
        check_vma=False,
    )
```

```python
import functools
import itertools

import jax
import jax.numpy as jnp
from jax import lax
from jax.experimental import pallas as pl
from jax.experimental.pallas import tpu as pltpu
from jax.sharding import PartitionSpec as P

TR = 32
BANDS = 32
CAP = 4
SUB = 8
LANES = 128
CHUNKS = 4
GREET_ALL = False
MESH = pl.DeviceIdType.MESH
F32 = jnp.float32
I32 = jnp.int32
BF16 = jnp.bfloat16
ROWS = (((1,), (0,)), ((), ()))


def iota(shape, dim):
    return lax.broadcasted_iota(I32, shape, dim)


def split(x):
    high = x.astype(BF16)
    return high, (x - high.astype(F32)).astype(BF16)


def dot(a, b, dims=ROWS):
    return lax.dot_general(a, b, dims, preferred_element_type=F32)


def total_of(terms):
    terms = list(terms)
    while len(terms) > 1:
        terms = [a + b for a, b in zip(terms[::2], terms[1::2])] + terms[len(terms) & ~1 :]
    return terms[0]


def by_distance(sizes):
    every = itertools.product(*(range(n) for n in sizes))
    return sorted(
        (step for step in every if any(step)),
        key=lambda step: (-sum(min(k, n - k) for k, n in zip(step, sizes) if n > 2), -step[-1], step),
    )


def back(steps, step, sizes):
    return steps.index(tuple((n - k) % n for k, n in zip(step, sizes)))


def kernel(
    groups, nx, nz, tiles,
    values_hbm, segments_hbm, rows_hbm, counts_hbm,
    rows_out, columns_out,
    values, segments, bands, counts, order_vmem, order,
    send_m, recv_m, send_a, recv_a, send_z, recv_z, send_x, recv_x, send_s, recv_s,
    send_b, recv_b, send_c, recv_c, send_r, recv_r,
    load_sem, small_sem, order_sem, send_sem, recv_sem,
):
    blocks = nx * nz
    half = groups // 2
    slots = groups * SUB
    me_g = lax.axis_index("grp")
    me_b = lax.axis_index("blk")
    me_y = me_g // 2
    me_x = me_b // nz
    me_z = me_b % nz
    per = tiles // CHUNKS

    group_steps = by_distance((half, 2))
    x_steps = by_distance((nx,))
    z_steps = by_distance((nz,))
    block_steps = by_distance((nx, nz))

    def group_device(step):
        return (lax.rem(me_y + step[0], half) * 2 + lax.rem(me_g + step[1], 2), me_b)

    def x_device(step):
        return (me_g, lax.rem(me_x + step[0], nx) * nz + me_z)

    def z_device(step):
        return (me_g, me_x * nz + lax.rem(me_z + step[0], nz))

    def block_device(step):
        return (me_g, lax.rem(me_x + step[0], nx) * nz + lax.rem(me_z + step[1], nz))

    def load(q):
        part = pl.ds(q * per, per)
        return pltpu.make_async_copy(values_hbm.at[part], values.at[part], load_sem.at[q])

    smalls = [
        pltpu.make_async_copy(src, dst, small_sem.at[n])
        for n, (src, dst) in enumerate(((segments_hbm, segments), (rows_hbm, bands), (counts_hbm, counts)))
    ]
    for copy in smalls:
        copy.start()
    for q in range(CHUNKS):
        load(q).start()

    empty = jnp.zeros((groups, SUB, LANES), F32)
    recv_a[...] = empty
    recv_c[...] = empty
    recv_m[...] = empty - 1.0

    barrier = pltpu.get_barrier_semaphore()
    greeted = [group_device(k) for k in group_steps]
    if GREET_ALL:
        greeted += [block_device(k) for k in block_steps]
    else:
        greeted += [z_device(k) for k in z_steps] + [x_device(k) for k in x_steps]
    for device in greeted:
        pl.semaphore_signal(barrier, inc=1, device_id=device, device_id_type=MESH)

    def send(stage, source, target, device):
        pltpu.make_async_remote_copy(
            src_ref=source, dst_ref=target, send_sem=send_sem.at[stage], recv_sem=recv_sem.at[stage],
            device_id=device, device_id_type=MESH,
        ).start()

    def finish(sem, stage, ref):
        pltpu.make_async_copy(ref, ref, sem.at[stage]).wait()

    def quad(ref):
        return ref.at[pl.ds(0, CAP)]

    def quads(ref):
        return ref.at[pl.ds(0, groups - 1), pl.ds(0, CAP)]

    def send_group(stage, source, target, n):
        step = group_steps[n]
        send(stage, quad(source.at[n]), quad(target.at[back(group_steps, step, (half, 2))]), group_device(step))

    def keep(source, target):
        target[groups - 1, :CAP] = source[groups - 1, :CAP]

    for copy in smalls:
        copy.wait()

    def at_place(code, steps, sizes):
        place = jnp.full(code.shape, len(steps), I32)
        for n, step in enumerate(steps):
            number = 0
            for k, size in zip(step, sizes):
                number = number * size + k
            place = jnp.where(code == number, n, place)
        return place

    seg = segments[...].reshape(1, tiles)
    count = counts[...].reshape(1, 1)
    group = seg // blocks
    block = seg % blocks
    group_code = (group // 2 + (half - me_y)) % half * 2 + (group + me_g) % 2
    group_row = at_place(group_code, group_steps, (half, 2)).astype(F32)
    z_place = at_place((block % nz + (nz - me_z)) % nz, z_steps, (nz,))
    block_row = (z_place * nx + block // nz).astype(F32)
    band_row = (bands[...].reshape(1, tiles) // TR).astype(F32)
    square = (tiles, tiles)
    down, along = iota(square, 0), iota(square, 1)
    diagonal = down == along

    def column(row):
        return jnp.sum(jnp.where(diagonal, row, 0.0), axis=1, keepdims=True)

    group_col = column(group_row)
    band_col = column(band_row)
    same_group = jnp.where(group_col == group_row, 1.0, 0.0)
    rank_row = jnp.sum(jnp.where(down < along, same_group, 0.0), axis=0, keepdims=True)
    rank_col = jnp.sum(jnp.where(along < down, same_group, 0.0), axis=1, keepdims=True)
    place_row = group_row * SUB + rank_row
    place_col = group_col * CAP + rank_col
    here = place_col == along.astype(F32)
    order_row = jnp.clip(jnp.sum(jnp.where(here, down, 0), axis=0, keepdims=True), 0, tiles - 1)
    order_vmem[:, :tiles] = order_row
    order_copy = pltpu.make_async_copy(order_vmem, order, order_sem)
    order_copy.start()
    slot_band = jnp.sum(jnp.where(here, band_col, 0.0), axis=0, keepdims=True)
    live_slot = order_row < count
    same_band = jnp.where((band_col == slot_band) & (down < count), 1.0, 0.0).astype(BF16)
    block_ids = jnp.sum(
        jnp.where(place_row == iota((slots, tiles), 0).astype(F32), block_row, 0.0), axis=1, keepdims=True
    )
    send_m[...] = jnp.broadcast_to(block_ids, (slots, LANES)).reshape(groups, SUB, LANES)
    keep(send_m, recv_m)

    lane = iota((TR, tiles), 1)

    def row_sums(tile_of):
        total = jnp.zeros((TR, tiles), F32)
        for t in range(tiles):
            total = jnp.where(lane == t, jnp.sum(tile_of(t), axis=1, keepdims=True), total)
        return total

    def row_scales(sums, members):
        high, low = split(sums)
        return jnp.where(live_slot, 1.0 / (dot(high, members) + dot(low, members)), 0.0)

    def column_pass(stage, weights, source, target):
        for n in range(groups):
            for k in range(CAP):
                s = n * CAP + k
                source[n, k : k + 1, :] = jnp.sum(
                    values[order[0, s]] * weights[:, s : s + 1], axis=0, keepdims=True
                )
            if n < groups - 1:
                send_group(stage, source, target, n)
        keep(source, target)

    def first(t):
        if t % per == 0:
            load(t // per).wait()
        return values[t]

    weights = row_scales(row_sums(first), same_band)
    order_copy.wait()
    pl.semaphore_wait(barrier, len(greeted))
    for n in range(groups - 1):
        send_group(0, send_m, recv_m, n)
    column_pass(1, weights, send_a, recv_a)

    slot_live_col = column(order_row.astype(F32)) < count.astype(F32)
    same_slot_band = jnp.where((column(slot_band) == slot_band) & slot_live_col, 1.0, 0.0).astype(BF16)
    finish(recv_sem, 0, quads(recv_m))
    ids = recv_m[...].reshape(slots, LANES)
    named = jnp.where(ids == iota((slots, LANES), 1).astype(F32), 1.0, 0.0)
    spread = named.T[:blocks].astype(BF16)
    named = named[:, :blocks].astype(BF16)

    def dense_of(ref):
        high, low = split(ref[...].reshape(slots, LANES))
        return dot(spread, high) + dot(spread, low)

    def others(ref):
        return ref.at[pl.ds(0, ref.shape[0] - 1)]

    finish(recv_sem, 1, quads(recv_a))
    send_z[...] = dense_of(recv_a).reshape(nz, nx, LANES)
    for n, step in enumerate(z_steps):
        send(2, send_z.at[n], recv_z.at[back(z_steps, step, (nz,))], z_device(step))
    recv_z[nz - 1] = send_z[nz - 1]
    finish(recv_sem, 2, others(recv_z))
    mine = total_of(recv_z[k] for k in range(nz))
    send_x[...] = mine
    for step in x_steps:
        send(3, send_x, recv_x.at[back(x_steps, step, (nx,))], x_device(step))
    recv_x[nx - 1] = mine
    finish(recv_sem, 3, others(recv_x))
    target = float(BANDS * TR) / LANES
    mine = target / total_of(recv_x[k] for k in range(nx))
    send_s[...] = mine
    for step in z_steps:
        send(4, send_s, recv_s.at[back(z_steps, step, (nz,))], z_device(step))
    recv_s[nz - 1] = mine
    finish(recv_sem, 4, others(recv_s))
    high, low = split(recv_s[...].reshape(blocks, LANES))
    send_b[...] = (dot(named, high) + dot(named, low)).reshape(groups, SUB, LANES)
    for n in range(groups - 1):
        send_group(5, send_b, recv_b, n)
    keep(send_b, recv_b)
    finish(recv_sem, 5, quads(recv_b))

    sums = row_sums(lambda s: values[order[0, s]] * recv_b[s // CAP, s % CAP : s % CAP + 1, :])
    column_pass(6, row_scales(sums, same_slot_band), send_c, recv_c)

    fold = LANES // TR
    lines = BANDS // fold
    high, low = split(jnp.concatenate([sums] * fold, axis=0))
    lane_part = iota((lines, LANES), 1) // TR
    band_sums = jnp.zeros((lines, LANES), F32)
    across = (((1,), (1,)), ((), ()))
    for m in range(fold):
        band = iota((lines, tiles), 0) * fold + m
        members = jnp.where((slot_band == band.astype(F32)) & live_slot, 1.0, 0.0).astype(BF16)
        band_sums = jnp.where(lane_part == m, dot(members, high, across) + dot(members, low, across), band_sums)
    rows_out[...] = 1.0 / band_sums

    finish(recv_sem, 6, quads(recv_c))
    send_r[...] = dense_of(recv_c).reshape(send_r.shape)
    z_offsets = [k for (k,) in z_steps] + [0]
    for n, step in enumerate(block_steps):
        row = z_offsets.index(step[1]) * nx + lax.rem(me_x + step[0], nx)
        send(7, send_r.at[pl.ds(row, 1)], recv_r.at[pl.ds(back(block_steps, step, (nx, nz)), 1)], block_device(step))
    recv_r[pl.ds(blocks - 1, 1)] = send_r[pl.ds((nz - 1) * nx + me_x, 1)]
    finish(recv_sem, 7, others(recv_r))
    columns_out[...] = target / jnp.sum(recv_r[...], axis=0, keepdims=True)

    for stage, ref in enumerate(
        (quads(recv_m), quads(recv_a), others(recv_z), others(recv_x), others(recv_s), quads(recv_b), quads(recv_c),
         others(recv_r))
    ):
        finish(send_sem, stage, ref)


def per_device(nx, nz, tile_values, tile_segments, tile_rows, tile_counts):
    groups = lax.axis_size("grp")
    blocks = lax.axis_size("blk")
    tiles = tile_values.shape[0]
    anywhere = pl.BlockSpec(memory_space=pltpu.HBM)
    group_buf = pltpu.VMEM((groups, SUB, LANES), F32)
    z_buf = pltpu.VMEM((nz, nx, LANES), F32)
    x_buf = pltpu.VMEM((nx, nx, LANES), F32)
    tile_buf = pltpu.VMEM((nx, LANES), F32)
    row_buf = pltpu.VMEM((blocks, LANES), F32)
    rows, columns = pl.pallas_call(
        functools.partial(kernel, groups, nx, nz, tiles),
        out_shape=(
            jax.ShapeDtypeStruct((BANDS * TR // LANES, LANES), F32),
            jax.ShapeDtypeStruct((1, LANES), F32),
        ),
        in_specs=[anywhere] * 4,
        out_specs=(pl.BlockSpec(memory_space=pltpu.VMEM),) * 2,
        scratch_shapes=[
            pltpu.VMEM((tiles, TR, LANES), F32),
            pltpu.VMEM((tiles,), I32),
            pltpu.VMEM((tiles,), I32),
            pltpu.VMEM((1,), I32),
            pltpu.VMEM((1, LANES), I32),
            pltpu.SMEM((1, LANES), I32),
            group_buf, group_buf, group_buf, group_buf,
            z_buf, z_buf, tile_buf, x_buf, tile_buf, z_buf,
            group_buf, group_buf, group_buf, group_buf,
            row_buf, row_buf,
            pltpu.SemaphoreType.DMA((CHUNKS,)),
            pltpu.SemaphoreType.DMA((3,)),
            pltpu.SemaphoreType.DMA,
            pltpu.SemaphoreType.DMA((8,)),
            pltpu.SemaphoreType.DMA((8,)),
        ],
        compiler_params=pltpu.CompilerParams(
            collective_id=0, has_side_effects=True, vmem_limit_bytes=53 * 1024 * 1024
        ),
    )(
        tile_values,
        tile_segments,
        tile_rows,
        tile_counts,
    )
    return rows.reshape(BANDS * TR), columns


def solution(mesh):
    blocks = mesh.shape["blk"]
    nz = 8
    nx = blocks // nz
    placed = (
        P(("grp", "blk"), None, None),
        P(("grp", "blk")),
        P(("grp", "blk")),
        P(("grp", "blk")),
    )
    return jax.shard_map(
        functools.partial(per_device, nx, nz),
        mesh=mesh,
        in_specs=placed,
        out_specs=(P(("grp", "blk")), P(("grp", "blk"), None)),
        check_vma=False,
    )
```

```python
import functools
import itertools

import jax
import jax.numpy as jnp
from jax import lax
from jax.experimental import pallas as pl
from jax.experimental.pallas import tpu as pltpu
from jax.sharding import PartitionSpec as P

TR = 32
BANDS = 32
CAP = 4
SUB = 8
LANES = 128
CHUNKS = 4
GREET_ALL = False
MESH = pl.DeviceIdType.MESH
F32 = jnp.float32
I32 = jnp.int32
BF16 = jnp.bfloat16
ROWS = (((1,), (0,)), ((), ()))


def iota(shape, dim):
    return lax.broadcasted_iota(I32, shape, dim)


def split(x):
    high = x.astype(BF16)
    return high, (x - high.astype(F32)).astype(BF16)


def dot(a, b, dims=ROWS):
    return lax.dot_general(a, b, dims, preferred_element_type=F32)


def total_of(terms):
    terms = list(terms)
    while len(terms) > 1:
        terms = [a + b for a, b in zip(terms[::2], terms[1::2])] + terms[len(terms) & ~1 :]
    return terms[0]


def by_distance(sizes):
    every = itertools.product(*(range(n) for n in sizes))
    return sorted(
        (step for step in every if any(step)),
        key=lambda step: (-sum(min(k, n - k) for k, n in zip(step, sizes) if n > 2), -step[-1], step),
    )


def back(steps, step, sizes):
    return steps.index(tuple((n - k) % n for k, n in zip(step, sizes)))


def kernel(
    groups, nx, nz, tiles,
    values_hbm, segments, bands, counts,
    rows_out, columns_out,
    values, order_vmem, order,
    send_m, recv_m, send_a, recv_a, send_z, recv_z, send_x, recv_x, send_s, recv_s,
    send_b, recv_b, send_c, recv_c, send_r, recv_r,
    load_sem, order_sem, send_sem, recv_sem,
):
    blocks = nx * nz
    half = groups // 2
    slots = groups * SUB
    me_g = lax.axis_index("grp")
    me_b = lax.axis_index("blk")
    me_y = me_g // 2
    me_x = me_b // nz
    me_z = me_b % nz
    per = tiles // CHUNKS

    group_steps = by_distance((half, 2))
    x_steps = by_distance((nx,))
    z_steps = by_distance((nz,))
    block_steps = by_distance((nx, nz))

    def group_device(step):
        return (lax.rem(me_y + step[0], half) * 2 + lax.rem(me_g + step[1], 2), me_b)

    def x_device(step):
        return (me_g, lax.rem(me_x + step[0], nx) * nz + me_z)

    def z_device(step):
        return (me_g, me_x * nz + lax.rem(me_z + step[0], nz))

    def block_device(step):
        return (me_g, lax.rem(me_x + step[0], nx) * nz + lax.rem(me_z + step[1], nz))

    def load(q):
        part = pl.ds(q * per, per)
        return pltpu.make_async_copy(values_hbm.at[part], values.at[part], load_sem.at[q])

    for q in range(CHUNKS):
        load(q).start()

    empty = jnp.zeros((groups, SUB, LANES), F32)
    recv_a[...] = empty
    recv_c[...] = empty
    recv_m[...] = empty - 1.0

    barrier = pltpu.get_barrier_semaphore()
    greeted = [group_device(k) for k in group_steps]
    if GREET_ALL:
        greeted += [block_device(k) for k in block_steps]
    else:
        greeted += [z_device(k) for k in z_steps] + [x_device(k) for k in x_steps]
    for device in greeted:
        pl.semaphore_signal(barrier, inc=1, device_id=device, device_id_type=MESH)

    def send(stage, source, target, device):
        pltpu.make_async_remote_copy(
            src_ref=source, dst_ref=target, send_sem=send_sem.at[stage], recv_sem=recv_sem.at[stage],
            device_id=device, device_id_type=MESH,
        ).start()

    def finish(sem, stage, ref):
        pltpu.make_async_copy(ref, ref, sem.at[stage]).wait()

    def quad(ref):
        return ref.at[pl.ds(0, CAP)]

    def quads(ref):
        return ref.at[pl.ds(0, groups - 1), pl.ds(0, CAP)]

    def send_group(stage, source, target, n):
        step = group_steps[n]
        send(stage, quad(source.at[n]), quad(target.at[back(group_steps, step, (half, 2))]), group_device(step))

    def keep(source, target):
        target[groups - 1, :CAP] = source[groups - 1, :CAP]


    def at_place(code, steps, sizes):
        place = jnp.full(code.shape, len(steps), I32)
        for n, step in enumerate(steps):
            number = 0
            for k, size in zip(step, sizes):
                number = number * size + k
            place = jnp.where(code == number, n, place)
        return place

    seg = segments[...].reshape(1, tiles)
    count = counts[...].reshape(1, 1)
    group = seg // blocks
    block = seg % blocks
    group_code = (group // 2 + (half - me_y)) % half * 2 + (group + me_g) % 2
    group_row = at_place(group_code, group_steps, (half, 2)).astype(F32)
    block_row = (block % nz * nx + block // nz).astype(F32)
    band_row = (bands[...].reshape(1, tiles) // TR).astype(F32)
    square = (tiles, tiles)
    down, along = iota(square, 0), iota(square, 1)
    diagonal = down == along

    def column(row):
        return jnp.sum(jnp.where(diagonal, row, 0.0), axis=1, keepdims=True)

    group_col = column(group_row)
    band_col = column(band_row)
    same_group = jnp.where(group_col == group_row, 1.0, 0.0)
    rank_row = jnp.sum(jnp.where(down < along, same_group, 0.0), axis=0, keepdims=True)
    rank_col = jnp.sum(jnp.where(along < down, same_group, 0.0), axis=1, keepdims=True)
    place_row = group_row * SUB + rank_row
    place_col = group_col * CAP + rank_col
    here = place_col == along.astype(F32)
    order_row = jnp.clip(jnp.sum(jnp.where(here, down, 0), axis=0, keepdims=True), 0, tiles - 1)
    order_vmem[:, :tiles] = order_row
    order_copy = pltpu.make_async_copy(order_vmem, order, order_sem)
    order_copy.start()
    slot_band = jnp.sum(jnp.where(here, band_col, 0.0), axis=0, keepdims=True)
    live_slot = order_row < count
    same_band = jnp.where((band_col == slot_band) & (down < count), 1.0, 0.0).astype(BF16)
    block_ids = jnp.sum(
        jnp.where(place_row == iota((slots, tiles), 0).astype(F32), block_row, 0.0), axis=1, keepdims=True
    )
    send_m[...] = jnp.broadcast_to(block_ids, (slots, LANES)).reshape(groups, SUB, LANES)
    keep(send_m, recv_m)

    lane = iota((TR, tiles), 1)

    def row_sums(tile_of):
        total = jnp.zeros((TR, tiles), F32)
        for t in range(tiles):
            total = jnp.where(lane == t, jnp.sum(tile_of(t), axis=1, keepdims=True), total)
        return total

    def row_scales(sums, members):
        high, low = split(sums)
        return jnp.where(live_slot, 1.0 / (dot(high, members) + dot(low, members)), 0.0)

    def column_pass(stage, weights, source, target):
        for n in range(groups):
            for k in range(CAP):
                s = n * CAP + k
                source[n, k : k + 1, :] = jnp.sum(
                    values[order[0, s]] * weights[:, s : s + 1], axis=0, keepdims=True
                )
            if n < groups - 1:
                send_group(stage, source, target, n)
        keep(source, target)

    def first(t):
        if t % per == 0:
            load(t // per).wait()
        return values[t]

    weights = row_scales(row_sums(first), same_band)
    order_copy.wait()
    pl.semaphore_wait(barrier, len(greeted))
    for n in range(groups - 1):
        send_group(0, send_m, recv_m, n)
    column_pass(1, weights, send_a, recv_a)

    slot_live_col = column(order_row.astype(F32)) < count.astype(F32)
    same_slot_band = jnp.where((column(slot_band) == slot_band) & slot_live_col, 1.0, 0.0).astype(BF16)
    finish(recv_sem, 0, quads(recv_m))
    ids = recv_m[...].reshape(slots, LANES)
    named = jnp.where(ids == iota((slots, LANES), 1).astype(F32), 1.0, 0.0)
    spread = named.T[:blocks].astype(BF16)
    named = named[:, :blocks].astype(BF16)

    def dense_of(ref):
        high, low = split(ref[...].reshape(slots, LANES))
        return dot(spread, high) + dot(spread, low)

    def others(ref):
        return ref.at[pl.ds(0, ref.shape[0] - 1)]

    planes = nz // 2
    target = float(BANDS * TR) / LANES
    sums_here = me_z >= planes
    finish(recv_sem, 1, quads(recv_a))
    send_z[...] = dense_of(recv_a).reshape(send_z.shape)
    for n in range(planes):

        @pl.when(me_z != planes + n)
        def _(n=n):
            send(2, send_z.at[n], recv_z.at[me_z], (me_g, me_x * nz + planes + n))

    @pl.when(sums_here)
    def _():
        recv_z[me_z] = send_z[me_z - planes]
        finish(recv_sem, 2, others(recv_z))
        mine = total_of(recv_z[k] for k in range(nz))
        send_x[...] = mine
        for step in x_steps:
            send(3, send_x, recv_x.at[back(x_steps, step, (nx,))], x_device(step))
        recv_x[nx - 1] = mine
        finish(recv_sem, 3, others(recv_x))
        mine = target / total_of(recv_x[k] for k in range(nx))
        send_s[...] = mine
        for step in z_steps:
            send(4, send_s, recv_s.at[me_z - planes], z_device(step))
        recv_s[me_z - planes] = mine
        finish(recv_sem, 4, others(recv_s))

    @pl.when(jnp.logical_not(sums_here))
    def _():
        finish(recv_sem, 4, recv_s)

    high, low = split(recv_s[...].reshape(blocks, LANES))
    send_b[...] = (dot(named, high) + dot(named, low)).reshape(groups, SUB, LANES)
    for n in range(groups - 1):
        send_group(5, send_b, recv_b, n)
    keep(send_b, recv_b)
    finish(recv_sem, 5, quads(recv_b))

    sums = row_sums(lambda s: values[order[0, s]] * recv_b[s // CAP, s % CAP : s % CAP + 1, :])
    column_pass(6, row_scales(sums, same_slot_band), send_c, recv_c)

    fold = LANES // TR
    lines = BANDS // fold
    high, low = split(jnp.concatenate([sums] * fold, axis=0))
    lane_part = iota((lines, LANES), 1) // TR
    band_sums = jnp.zeros((lines, LANES), F32)
    across = (((1,), (1,)), ((), ()))
    for m in range(fold):
        band = iota((lines, tiles), 0) * fold + m
        members = jnp.where((slot_band == band.astype(F32)) & live_slot, 1.0, 0.0).astype(BF16)
        band_sums = jnp.where(lane_part == m, dot(members, high, across) + dot(members, low, across), band_sums)
    rows_out[...] = 1.0 / band_sums

    finish(recv_sem, 6, quads(recv_c))
    send_r[...] = dense_of(recv_c).reshape(send_r.shape)
    for n, step in enumerate(block_steps):
        row = lax.rem(me_z + step[1], nz) * nx + lax.rem(me_x + step[0], nx)
        send(7, send_r.at[pl.ds(row, 1)], recv_r.at[pl.ds(back(block_steps, step, (nx, nz)), 1)], block_device(step))
    recv_r[pl.ds(blocks - 1, 1)] = send_r[pl.ds(me_z * nx + me_x, 1)]
    finish(recv_sem, 7, others(recv_r))
    columns_out[...] = target / jnp.sum(recv_r[...], axis=0, keepdims=True)

    for stage, ref in ((0, quads(recv_m)), (1, quads(recv_a)), (5, quads(recv_b)), (6, quads(recv_c)), (7, others(recv_r))):
        finish(send_sem, stage, ref)

    @pl.when(sums_here)
    def _():
        finish(send_sem, 2, others(send_z))
        finish(send_sem, 3, others(recv_x))
        finish(send_sem, 4, others(recv_z))

    @pl.when(jnp.logical_not(sums_here))
    def _():
        finish(send_sem, 2, send_z)


def per_device(nx, nz, tile_values, tile_segments, tile_rows, tile_counts):
    groups = lax.axis_size("grp")
    blocks = lax.axis_size("blk")
    tiles = tile_values.shape[0]
    anywhere = pl.BlockSpec(memory_space=pltpu.HBM)
    group_buf = pltpu.VMEM((groups, SUB, LANES), F32)
    double = 2 * nx
    plane_buf = pltpu.VMEM((nz // 2, double, LANES), F32)
    z_buf = pltpu.VMEM((nz, double, LANES), F32)
    x_buf = pltpu.VMEM((nx, double, LANES), F32)
    tile_buf = pltpu.VMEM((double, LANES), F32)
    row_buf = pltpu.VMEM((blocks, LANES), F32)
    rows, columns = pl.pallas_call(
        functools.partial(kernel, groups, nx, nz, tiles),
        out_shape=(
            jax.ShapeDtypeStruct((BANDS * TR // LANES, LANES), F32),
            jax.ShapeDtypeStruct((1, LANES), F32),
        ),
        in_specs=[anywhere] + [pl.BlockSpec(memory_space=pltpu.VMEM)] * 3,
        out_specs=(pl.BlockSpec(memory_space=pltpu.VMEM),) * 2,
        scratch_shapes=[
            pltpu.VMEM((tiles, TR, LANES), F32),
            pltpu.VMEM((1, LANES), I32),
            pltpu.SMEM((1, LANES), I32),
            group_buf, group_buf, group_buf, group_buf,
            plane_buf, z_buf, tile_buf, x_buf, tile_buf, plane_buf,
            group_buf, group_buf, group_buf, group_buf,
            row_buf, row_buf,
            pltpu.SemaphoreType.DMA((CHUNKS,)),
            pltpu.SemaphoreType.DMA,
            pltpu.SemaphoreType.DMA((8,)),
            pltpu.SemaphoreType.DMA((8,)),
        ],
        compiler_params=pltpu.CompilerParams(
            collective_id=0, has_side_effects=True, vmem_limit_bytes=53 * 1024 * 1024
        ),
    )(
        tile_values,
        tile_segments,
        tile_rows,
        tile_counts,
    )
    return rows.reshape(BANDS * TR), columns


def solution(mesh):
    blocks = mesh.shape["blk"]
    nz = 8
    nx = blocks // nz
    placed = (
        P(("grp", "blk"), None, None),
        P(("grp", "blk")),
        P(("grp", "blk")),
        P(("grp", "blk")),
    )
    return jax.shard_map(
        functools.partial(per_device, nx, nz),
        mesh=mesh,
        in_specs=placed,
        out_specs=(P(("grp", "blk")), P(("grp", "blk"), None)),
        check_vma=False,
    )
```

```python
import functools
import itertools

import jax
import jax.numpy as jnp
from jax import lax
from jax.experimental import pallas as pl
from jax.experimental.pallas import tpu as pltpu
from jax.sharding import PartitionSpec as P

TR = 32
BANDS = 32
CAP = 4
SUB = 8
LANES = 128
CHUNKS = 4
GREET_ALL = False
MESH = pl.DeviceIdType.MESH
F32 = jnp.float32
I32 = jnp.int32
BF16 = jnp.bfloat16
ROWS = (((1,), (0,)), ((), ()))


def iota(shape, dim):
    return lax.broadcasted_iota(I32, shape, dim)


def split(x):
    high = x.astype(BF16)
    return high, (x - high.astype(F32)).astype(BF16)


def dot(a, b, dims=ROWS):
    return lax.dot_general(a, b, dims, preferred_element_type=F32)


def total_of(terms):
    terms = list(terms)
    while len(terms) > 1:
        terms = [a + b for a, b in zip(terms[::2], terms[1::2])] + terms[len(terms) & ~1 :]
    return terms[0]


def by_distance(sizes):
    every = itertools.product(*(range(n) for n in sizes))
    return sorted(
        (step for step in every if any(step)),
        key=lambda step: (-sum(min(k, n - k) for k, n in zip(step, sizes) if n > 2), -step[-1], step),
    )


def back(steps, step, sizes):
    return steps.index(tuple((n - k) % n for k, n in zip(step, sizes)))


def kernel(
    groups, nx, nz, tiles,
    values_hbm, segments, bands, counts,
    rows_out, columns_out,
    values, order_vmem, order,
    send_m, recv_m, send_a, recv_a, send_z, recv_z, send_x, recv_x, send_s, recv_s,
    send_b, recv_b, send_c, recv_c, send_r, recv_r,
    load_sem, order_sem, send_sem, recv_sem,
):
    blocks = nx * nz
    half = groups // 2
    slots = groups * SUB
    me_g = lax.axis_index("grp")
    me_b = lax.axis_index("blk")
    me_y = me_g // 2
    me_x = me_b // nz
    me_z = me_b % nz
    per = tiles // CHUNKS

    group_steps = by_distance((half, 2))
    x_steps = by_distance((nx,))
    z_steps = by_distance((nz,))
    block_steps = by_distance((nx, nz))

    def group_device(step):
        return (lax.rem(me_y + step[0], half) * 2 + lax.rem(me_g + step[1], 2), me_b)

    def x_device(step):
        return (me_g, lax.rem(me_x + step[0], nx) * nz + me_z)

    def z_device(step):
        return (me_g, me_x * nz + lax.rem(me_z + step[0], nz))

    def block_device(step):
        return (me_g, lax.rem(me_x + step[0], nx) * nz + lax.rem(me_z + step[1], nz))

    def load(q):
        part = pl.ds(q * per, per)
        return pltpu.make_async_copy(values_hbm.at[part], values.at[part], load_sem.at[q])

    for q in range(CHUNKS):
        load(q).start()

    empty = jnp.zeros((groups, SUB, LANES), F32)
    recv_a[...] = empty
    recv_c[...] = empty
    recv_m[...] = empty - 1.0

    barrier = pltpu.get_barrier_semaphore()
    greeted = [group_device(k) for k in group_steps]
    if GREET_ALL:
        greeted += [block_device(k) for k in block_steps]
    else:
        greeted += [z_device(k) for k in z_steps] + [x_device(k) for k in x_steps]
    for device in greeted:
        pl.semaphore_signal(barrier, inc=1, device_id=device, device_id_type=MESH)

    def send(stage, source, target, device):
        pltpu.make_async_remote_copy(
            src_ref=source, dst_ref=target, send_sem=send_sem.at[stage], recv_sem=recv_sem.at[stage],
            device_id=device, device_id_type=MESH,
        ).start()

    def finish(sem, stage, ref):
        pltpu.make_async_copy(ref, ref, sem.at[stage]).wait()

    def quad(ref):
        return ref.at[pl.ds(0, CAP)]

    def quads(ref):
        return ref.at[pl.ds(0, groups - 1), pl.ds(0, CAP)]

    def send_group(stage, source, target, n):
        step = group_steps[n]
        send(stage, quad(source.at[n]), quad(target.at[back(group_steps, step, (half, 2))]), group_device(step))

    def keep(source, target):
        target[groups - 1, :CAP] = source[groups - 1, :CAP]


    def at_place(code, steps, sizes):
        place = jnp.full(code.shape, len(steps), I32)
        for n, step in enumerate(steps):
            number = 0
            for k, size in zip(step, sizes):
                number = number * size + k
            place = jnp.where(code == number, n, place)
        return place

    seg = segments[...].reshape(1, tiles)
    count = counts[...].reshape(1, 1)
    group = seg // blocks
    block = seg % blocks
    group_code = (group // 2 + (half - me_y)) % half * 2 + (group + me_g) % 2
    group_row = at_place(group_code, group_steps, (half, 2)).astype(F32)
    block_row = (block % nz * nx + block // nz).astype(F32)
    band_row = (bands[...].reshape(1, tiles) // TR).astype(F32)
    square = (tiles, tiles)
    down, along = iota(square, 0), iota(square, 1)
    diagonal = down == along

    def column(row):
        return jnp.sum(jnp.where(diagonal, row, 0.0), axis=1, keepdims=True)

    group_col = column(group_row)
    band_col = column(band_row)
    same_group = jnp.where(group_col == group_row, 1.0, 0.0)
    rank_row = jnp.sum(jnp.where(down < along, same_group, 0.0), axis=0, keepdims=True)
    rank_col = jnp.sum(jnp.where(along < down, same_group, 0.0), axis=1, keepdims=True)
    place_row = group_row * SUB + rank_row
    place_col = group_col * CAP + rank_col
    here = place_col == along.astype(F32)
    order_row = jnp.clip(jnp.sum(jnp.where(here, down, 0), axis=0, keepdims=True), 0, tiles - 1)
    order_vmem[:, :tiles] = order_row
    order_copy = pltpu.make_async_copy(order_vmem, order, order_sem)
    order_copy.start()
    slot_band = jnp.sum(jnp.where(here, band_col, 0.0), axis=0, keepdims=True)
    live_slot = order_row < count
    same_band = jnp.where((band_col == slot_band) & (down < count), 1.0, 0.0).astype(BF16)
    block_ids = jnp.sum(
        jnp.where(place_row == iota((slots, tiles), 0).astype(F32), block_row, 0.0), axis=1, keepdims=True
    )
    send_m[...] = jnp.broadcast_to(block_ids, (slots, LANES)).reshape(groups, SUB, LANES)
    keep(send_m, recv_m)

    lane = iota((TR, tiles), 1)

    def row_sums(tile_of):
        total = jnp.zeros((TR, tiles), F32)
        for t in range(tiles):
            total = jnp.where(lane == t, jnp.sum(tile_of(t), axis=1, keepdims=True), total)
        return total

    def row_scales(sums, members):
        high, low = split(sums)
        return jnp.where(live_slot, 1.0 / (dot(high, members) + dot(low, members)), 0.0)

    def column_pass(stage, weights, source, target):
        for n in range(groups):
            for k in range(CAP):
                s = n * CAP + k
                source[n, k : k + 1, :] = jnp.sum(
                    values[order[0, s]] * weights[:, s : s + 1], axis=0, keepdims=True
                )
            if n < groups - 1:
                send_group(stage, source, target, n)
        keep(source, target)

    def first(t):
        if t % per == 0:
            load(t // per).wait()
        return values[t]

    weights = row_scales(row_sums(first), same_band)
    order_copy.wait()
    pl.semaphore_wait(barrier, len(greeted))
    for n in range(groups - 1):
        send_group(0, send_m, recv_m, n)
    column_pass(1, weights, send_a, recv_a)

    slot_live_col = column(order_row.astype(F32)) < count.astype(F32)
    same_slot_band = jnp.where((column(slot_band) == slot_band) & slot_live_col, 1.0, 0.0).astype(BF16)
    finish(recv_sem, 0, quads(recv_m))
    ids = recv_m[...].reshape(slots, LANES)
    named = jnp.where(ids == iota((slots, LANES), 1).astype(F32), 1.0, 0.0)
    spread = named.T[:blocks].astype(BF16)
    named = named[:, :blocks].astype(BF16)
    spread_twice = jnp.concatenate([spread, spread], axis=1)
    named_twice = jnp.concatenate([named, named], axis=1)

    def dense_of(ref):
        high, low = split(ref[...].reshape(slots, LANES))
        return dot(spread_twice, jnp.concatenate([high, low], axis=0))

    def others(ref):
        return ref.at[pl.ds(0, ref.shape[0] - 1)]

    planes = nz // 2
    target = float(BANDS * TR) / LANES
    sums_here = me_z >= planes
    finish(recv_sem, 1, quads(recv_a))
    send_z[...] = dense_of(recv_a).reshape(send_z.shape)
    for n in range(planes):

        @pl.when(me_z != planes + n)
        def _(n=n):
            send(2, send_z.at[n], recv_z.at[me_z], (me_g, me_x * nz + planes + n))

    @pl.when(sums_here)
    def _():
        recv_z[me_z] = send_z[me_z - planes]
        finish(recv_sem, 2, others(recv_z))
        mine = total_of(recv_z[k] for k in range(nz))
        send_x[...] = mine
        for step in x_steps:
            send(3, send_x, recv_x.at[back(x_steps, step, (nx,))], x_device(step))
        recv_x[nx - 1] = mine
        finish(recv_sem, 3, others(recv_x))
        mine = target / total_of(recv_x[k] for k in range(nx))
        send_s[...] = mine
        for step in z_steps:
            send(4, send_s, recv_s.at[me_z - planes], z_device(step))
        recv_s[me_z - planes] = mine
        finish(recv_sem, 4, others(recv_s))

    @pl.when(jnp.logical_not(sums_here))
    def _():
        finish(recv_sem, 4, recv_s)

    high, low = split(recv_s[...].reshape(blocks, LANES))
    send_b[...] = dot(named_twice, jnp.concatenate([high, low], axis=0)).reshape(groups, SUB, LANES)
    for n in range(groups - 1):
        send_group(5, send_b, recv_b, n)
    keep(send_b, recv_b)
    finish(recv_sem, 5, quads(recv_b))

    sums = row_sums(lambda s: values[order[0, s]] * recv_b[s // CAP, s % CAP : s % CAP + 1, :])
    column_pass(6, row_scales(sums, same_slot_band), send_c, recv_c)

    fold = LANES // TR
    lines = BANDS // fold
    high, low = split(jnp.concatenate([sums] * fold, axis=0))
    lane_part = iota((lines, LANES), 1) // TR
    band_sums = jnp.zeros((lines, LANES), F32)
    across = (((1,), (1,)), ((), ()))
    for m in range(fold):
        band = iota((lines, tiles), 0) * fold + m
        members = jnp.where((slot_band == band.astype(F32)) & live_slot, 1.0, 0.0).astype(BF16)
        band_sums = jnp.where(lane_part == m, dot(members, high, across) + dot(members, low, across), band_sums)
    rows_out[...] = 1.0 / band_sums

    finish(recv_sem, 6, quads(recv_c))
    send_r[...] = dense_of(recv_c).reshape(send_r.shape)
    for n, step in enumerate(block_steps):
        row = lax.rem(me_z + step[1], nz) * nx + lax.rem(me_x + step[0], nx)
        send(7, send_r.at[pl.ds(row, 1)], recv_r.at[pl.ds(back(block_steps, step, (nx, nz)), 1)], block_device(step))
    recv_r[pl.ds(blocks - 1, 1)] = send_r[pl.ds(me_z * nx + me_x, 1)]
    finish(recv_sem, 7, others(recv_r))
    columns_out[...] = target / jnp.sum(recv_r[...], axis=0, keepdims=True)

    for stage, ref in ((0, quads(recv_m)), (1, quads(recv_a)), (5, quads(recv_b)), (6, quads(recv_c)), (7, others(recv_r))):
        finish(send_sem, stage, ref)

    @pl.when(sums_here)
    def _():
        finish(send_sem, 2, others(send_z))
        finish(send_sem, 3, others(recv_x))
        finish(send_sem, 4, others(recv_z))

    @pl.when(jnp.logical_not(sums_here))
    def _():
        finish(send_sem, 2, send_z)


def per_device(nx, nz, tile_values, tile_segments, tile_rows, tile_counts):
    groups = lax.axis_size("grp")
    blocks = lax.axis_size("blk")
    tiles = tile_values.shape[0]
    anywhere = pl.BlockSpec(memory_space=pltpu.HBM)
    group_buf = pltpu.VMEM((groups, SUB, LANES), F32)
    double = 2 * nx
    plane_buf = pltpu.VMEM((nz // 2, double, LANES), F32)
    z_buf = pltpu.VMEM((nz, double, LANES), F32)
    x_buf = pltpu.VMEM((nx, double, LANES), F32)
    tile_buf = pltpu.VMEM((double, LANES), F32)
    row_buf = pltpu.VMEM((blocks, LANES), F32)
    rows, columns = pl.pallas_call(
        functools.partial(kernel, groups, nx, nz, tiles),
        out_shape=(
            jax.ShapeDtypeStruct((BANDS * TR // LANES, LANES), F32),
            jax.ShapeDtypeStruct((1, LANES), F32),
        ),
        in_specs=[anywhere] + [pl.BlockSpec(memory_space=pltpu.VMEM)] * 3,
        out_specs=(pl.BlockSpec(memory_space=pltpu.VMEM),) * 2,
        scratch_shapes=[
            pltpu.VMEM((tiles, TR, LANES), F32),
            pltpu.VMEM((1, LANES), I32),
            pltpu.SMEM((1, LANES), I32),
            group_buf, group_buf, group_buf, group_buf,
            plane_buf, z_buf, tile_buf, x_buf, tile_buf, plane_buf,
            group_buf, group_buf, group_buf, group_buf,
            row_buf, row_buf,
            pltpu.SemaphoreType.DMA((CHUNKS,)),
            pltpu.SemaphoreType.DMA,
            pltpu.SemaphoreType.DMA((8,)),
            pltpu.SemaphoreType.DMA((8,)),
        ],
        compiler_params=pltpu.CompilerParams(
            collective_id=0, has_side_effects=True, vmem_limit_bytes=53 * 1024 * 1024
        ),
    )(
        tile_values,
        tile_segments,
        tile_rows,
        tile_counts,
    )
    return rows.reshape(BANDS * TR), columns


def solution(mesh):
    blocks = mesh.shape["blk"]
    nz = 8
    nx = blocks // nz
    placed = (
        P(("grp", "blk"), None, None),
        P(("grp", "blk")),
        P(("grp", "blk")),
        P(("grp", "blk")),
    )
    return jax.shard_map(
        functools.partial(per_device, nx, nz),
        mesh=mesh,
        in_specs=placed,
        out_specs=(P(("grp", "blk")), P(("grp", "blk"), None)),
        check_vma=False,
    )
```
